32 devices in a mesh: groups: 2 (over x), expert: 16 (over z, y, core).
Axes of the slice: x: 2, y: 2, z: 4, core: 2. Of those that a mesh axis runs over, the one named last changes fastest.
Arguments:
- tokens: bfloat16 [4096, 7168], P(('groups', 'expert')), parts along dimension 0, may hold values from -6 to 6
- route_ids: int32 [4096, 8], P(('groups', 'expert')), parts along dimension 0, may hold values from 0 to 255, as said below
- gate_fixed: int32 [4096, 8], P(('groups', 'expert')), parts along dimension 0, may hold values from 1 to 32767
- capacity: int32 [4], P('groups'), parts along dimension 0, may hold values from 1 to 2, as said below
- placement: int32 [2, 3], P('groups'), parts along dimension 0, may hold values from 0 to 1, as said below
- gate_weight: bfloat16 [16, 7168, 128], P('expert'), may hold values from -0.0625 to 0.0625
- up_weight: bfloat16 [16, 7168, 128], P('expert'), may hold values from -0.0625 to 0.0625
- down_weight: bfloat16 [16, 7168, 128], P('expert'), may hold values from -0.1875 to 0.1875
Outputs:
- mixed: bfloat16 [4096, 7168], P(('groups', 'expert')), parts along dimension 0
The draws below stay inside these ranges and needn't reach their ends.
There are 2 independent parts, one for each index of `groups`. The reference program is written for one: setup_inputs(seed, part) draws one part's arguments, and reference() takes and returns one part's arrays. A program takes and returns all parts, laid end to end along the dimension named above; an argument that names none is the same for every part. Nothing has to cross between parts.
Inputs may be any that keep to these rules, and one draw needn't show every extreme that they name: `route_ids`: each row names 8 different experts. `capacity`: some slot accepts exactly 2. `placement`: expert ids are distinct and below 1; the old owner equals the expert id; new owners are distinct slots of 1 to 1.
All inputs are finite; a program needn't handle non-finite values.
Results may differ from the reference program's by a relative error of at most 0.0085.
Values may be sent and summed in bfloat16 or wider, within the bound.
No kernel may reach another device: no remote copies, remote signals or barrier semaphores. Data moves between devices by JAX's collectives and lax.ppermute only.
A program may use at most 64 MiB of HBM per device.

```python
import jax
import jax.numpy as jnp
from jax import lax

D = 7168
FF_W = 1024
HID_DEV = 128
ALL_EXP = 256
TOPK = 8
TOK_DEV = 128
GROUP = 8
SLOTS = 2
REPL = 1
LIVE = 1
CAP = 2
TOKENS = 2048
N_EXPERT = 16


def hot_experts(key):
    return jax.random.permutation(key, LIVE)[:REPL].astype(jnp.int32)


def draw_placement(key, part):
    hot_ids = hot_experts(key)
    key = jax.random.fold_in(key, 11)
    landing = (LIVE + jax.random.permutation(key, REPL)).astype(jnp.int32)
    return jnp.stack((hot_ids, landing, hot_ids), axis=1).astype(jnp.int32)


def draw_route_ids(key, part):
    hot_ids = hot_experts(key)
    key = jax.random.fold_in(key, 12)
    keys = jax.random.split(key, 3)
    shape_all = (TOKENS, ALL_EXP)
    first = jax.random.randint(keys[0], shape_all, 0, 1048576, dtype=jnp.int32)
    second = jax.random.randint(keys[1], shape_all, 0, 1048576, dtype=jnp.int32)
    third = jax.random.randint(keys[2], shape_all, 0, 1048576, dtype=jnp.int32)
    expert_index = jnp.arange(ALL_EXP, dtype=jnp.int32)
    is_hot = jnp.any(expert_index[:, None] == hot_ids[None, :], axis=1)
    score = jnp.where(is_hot[None, :], jnp.maximum(first, jnp.maximum(second, third)), first)
    score = score * ALL_EXP + expert_index[None, :]
    return lax.top_k(score, TOPK)[1].astype(jnp.int32)


def draw_capacity(key, part):
    key = jax.random.fold_in(key, 13)
    keys = jax.random.split(key, 2)
    values = jax.random.randint(keys[0], (SLOTS,), max(1, CAP // 2), CAP + 1, dtype=jnp.int32)
    full_at = jax.random.randint(keys[1], (), 0, SLOTS, dtype=jnp.int32)
    return jnp.where(jnp.arange(SLOTS, dtype=jnp.int32) == full_at, CAP, values).astype(jnp.int32)


def touch_ends(result, stream_key, low, high):
    longest = result.shape.index(max(result.shape))
    spots = []
    for shift in (0, 1):
        where = [jax.random.randint(jax.random.fold_in(stream_key, axis), (), 0, length) for axis, length in enumerate(result.shape)]
        where[longest] = (where[longest] + shift) % result.shape[longest]
        spots.append(tuple(where))
    return result.at[spots[0]].set(low).at[spots[1]].set(high)


def block_scale(key, shape, cuts, least, top_value):
    def one(dim, blocks):
        draws = jax.random.uniform(jax.random.fold_in(jax.random.fold_in(key, 6), dim), (blocks,), jnp.float32, least / len(cuts), top_value / len(cuts))
        return jnp.repeat(jnp.exp(draws), shape[dim] // blocks).reshape((-1,) + (1,) * (len(shape) - dim - 1))

    loudness = one(*cuts[0])
    for cut in cuts[1:]:
        loudness = loudness * one(*cut)
    return loudness


def scatter_about(stream_key, extent, deviation, limit, cuts=(), held_as=jnp.bfloat16):
    values = deviation * jax.random.normal(stream_key, extent, jnp.float32)
    if cuts:
        values = values * block_scale(stream_key, extent, cuts, -0.22, 0.18)
    return jnp.clip(values, -limit, limit).astype(held_as)


def setup_inputs(seed: int = 0, part: int = 0) -> dict:
    streams_of = jax.random.split(jax.random.key(seed), 9)
    part_splits = jax.random.split(jax.random.fold_in(streams_of[8], part), 9)
    tokens = scatter_about(part_splits[0], (TOKENS, D), 1.0, 6.0, ((0, 16),))
    route_ids = draw_route_ids(jax.random.fold_in(jax.random.fold_in(streams_of[8], part), 71), part)
    gate_fixed = touch_ends(jax.random.randint(part_splits[2], (TOKENS, TOPK), 1, 32768), jax.random.fold_in(part_splits[2], 1), 1, 32767).astype(jnp.int32)
    capacity = draw_capacity(jax.random.fold_in(jax.random.fold_in(streams_of[8], part), 71), part)
    placement = draw_placement(jax.random.fold_in(jax.random.fold_in(streams_of[8], part), 71), part)
    gate_weight = scatter_about(streams_of[5], (SLOTS * GROUP, D, HID_DEV), D ** -0.5, 0.0625, ((0, 16),))
    up_weight = scatter_about(streams_of[6], (SLOTS * GROUP, D, HID_DEV), D ** -0.5, 0.0625, ((0, 16),))
    down_weight = scatter_about(streams_of[7], (SLOTS * GROUP, D, HID_DEV), FF_W ** -0.5, 0.1875, ((0, 16),))
    return {"tokens": tokens, "route_ids": route_ids, "gate_fixed": gate_fixed, "capacity": capacity, "placement": placement, "gate_weight": gate_weight, "up_weight": up_weight, "down_weight": down_weight}


GATE_UNIT = 1.0 / 32768.0


def slot_tables(placement, slot_count):
    old_slot = placement[:, 0]
    new_slot = placement[:, 1]
    expert_id = placement[:, 2]
    slot_range = jnp.arange(slot_count, dtype=jnp.int32)
    is_named = expert_id[None, :] == slot_range[:, None]
    has_copy = jnp.any(is_named, axis=1)
    copy_slot = jnp.sum(jnp.where(is_named, new_slot[None, :], 0), axis=1).astype(jnp.int32)
    landing = new_slot[None, :] == slot_range[:, None]
    source_slot = jnp.where(jnp.any(landing, axis=1), jnp.sum(jnp.where(landing, old_slot[None, :], 0), axis=1), slot_range).astype(jnp.int32)
    return has_copy, copy_slot, source_slot


def assign(route_ids, gate_fixed, capacity, has_copy, copy_slot, live_count, slot_rows):
    row_count = route_ids.shape[0]
    slot_count = capacity.shape[0]
    slot_range = jnp.arange(slot_count, dtype=jnp.int32)
    is_live = route_ids < live_count
    onehot = route_ids[:, :, None] == slot_range[None, None, :]
    doubled = jnp.any(onehot & has_copy[None, None, :], axis=2)
    copy_of = jnp.sum(jnp.where(onehot, copy_slot[None, None, :], 0), axis=2)
    odd_row = (jnp.arange(row_count, dtype=jnp.int32) % 2 == 1)[:, None]
    slot_of = jnp.where(doubled & odd_row, copy_of, jnp.where(is_live, route_ids, 0)).astype(jnp.int32)
    flat_slot = slot_of.reshape(-1)
    flat_live = is_live.reshape(-1)
    member = ((flat_slot[:, None] == slot_range[None, :]) & flat_live[:, None]).astype(jnp.int32)
    before = jnp.cumsum(member, axis=0) - member
    position = jnp.sum(before * member, axis=1)
    allowed = jnp.sum(member * capacity[None, :], axis=1)
    kept_pair = flat_live & (position < allowed)
    target = (flat_slot * slot_rows + position).astype(jnp.int32)
    weight = jnp.where(kept_pair, gate_fixed.reshape(-1).astype(jnp.float32) * GATE_UNIT, 0.0).astype(jnp.float32)
    return target, kept_pair, weight


def tables(target, kept_pair, weight, row_count, table_width):
    column = jnp.arange(table_width, dtype=jnp.int32)
    matches = (target[:, None] == column[None, :]) & kept_pair[:, None]
    chosen = jnp.sum(matches.astype(jnp.int32).reshape(row_count, -1, table_width), axis=1)
    mixing = jnp.sum((matches.astype(jnp.float32) * weight[:, None]).reshape(row_count, -1, table_width), axis=1)
    return chosen, mixing


def reference(tokens, route_ids, gate_fixed, capacity, placement, gate_weight, up_weight, down_weight):
    group_size = FF_W // HID_DEV
    slot_count = N_EXPERT // group_size
    live_count = slot_count - REPL
    model_width = tokens.shape[1]
    has_copy, copy_slot, source_slot = slot_tables(placement, slot_count)
    route_dev = route_ids.reshape(N_EXPERT, TOK_DEV, TOPK)
    fixed_dev = gate_fixed.reshape(N_EXPERT, TOK_DEV, TOPK)

    def per_device(ids_block, fixed_block):
        target, kept_pair, weight = assign(ids_block, fixed_block, capacity, has_copy, copy_slot, live_count, CAP)
        return tables(target, kept_pair, weight, TOK_DEV, slot_count * CAP)

    chosen, mixing = jax.vmap(per_device)(route_dev, fixed_dev)
    local_ids = jnp.arange(TOK_DEV, dtype=jnp.int32)
    token_of = jnp.sum(chosen * local_ids[None, :, None], axis=1).astype(jnp.int32)
    filled = jnp.sum(chosen, axis=1)
    token_dev = tokens.reshape(N_EXPERT, TOK_DEV, model_width)
    gathered = jnp.take_along_axis(token_dev, token_of[:, :, None], axis=1)
    gathered = jnp.where(filled[:, :, None] > 0, gathered, jnp.zeros((), jnp.bfloat16))
    gathered = gathered.reshape(N_EXPERT, slot_count, CAP, model_width).transpose(1, 0, 2, 3)
    gathered = gathered.reshape(slot_count, N_EXPERT * CAP, model_width)
    gate_all = gate_weight.reshape(slot_count, group_size, model_width, HID_DEV)
    up_all = up_weight.reshape(slot_count, group_size, model_width, HID_DEV)
    down_all = down_weight.reshape(slot_count, group_size, model_width, HID_DEV)

    def one_slot(inputs):
        slot_rows, source = inputs
        gate_full = jnp.transpose(gate_all[source], (1, 0, 2)).reshape(model_width, FF_W)
        up_full = jnp.transpose(up_all[source], (1, 0, 2)).reshape(model_width, FF_W)
        gate_val = jnp.dot(slot_rows, gate_full, preferred_element_type=jnp.float32)
        up_val = jnp.dot(slot_rows, up_full, preferred_element_type=jnp.float32)
        hidden = (jax.nn.silu(gate_val) * up_val).astype(jnp.bfloat16)
        blocks = hidden.reshape(-1, group_size, HID_DEV).astype(jnp.float32)
        partial_value = jnp.einsum('rgh,gdh->grd', blocks, down_all[source].astype(jnp.float32), precision=lax.Precision.HIGHEST)
        return jnp.sum(partial_value.astype(jnp.bfloat16).astype(jnp.float32), axis=0)

    outputs = lax.map(one_slot, (gathered, source_slot))
    outputs = outputs.reshape(slot_count, N_EXPERT, CAP, model_width).transpose(1, 0, 2, 3)
    outputs = outputs.reshape(N_EXPERT, slot_count * CAP, model_width)
    combined = jnp.einsum('nts,nsd->ntd', mixing, outputs, precision=lax.Precision.HIGHEST)
    return combined.reshape(TOKENS, model_width).astype(jnp.bfloat16)
```

```python
import jax
import jax.numpy as jnp
from jax import lax
from jax.experimental import pallas as pl
from jax.experimental.pallas import tpu as pltpu
from jax.sharding import PartitionSpec as P

FF_W = 1024
HID_DEV = 128
CAP = 2


GATE_UNIT = 1.0 / 32768.0


def slot_tables(placement, slot_count):
    old_slot = placement[:, 0]
    new_slot = placement[:, 1]
    expert_id = placement[:, 2]
    slot_range = jnp.arange(slot_count, dtype=jnp.int32)
    is_named = expert_id[None, :] == slot_range[:, None]
    has_copy = jnp.any(is_named, axis=1)
    copy_slot = jnp.sum(jnp.where(is_named, new_slot[None, :], 0), axis=1)
    landing = new_slot[None, :] == slot_range[:, None]
    source_slot = jnp.where(
        jnp.any(landing, axis=1),
        jnp.sum(jnp.where(landing, old_slot[None, :], 0), axis=1),
        slot_range,
    )
    return (has_copy, copy_slot, source_slot)


def assign(route_ids, gate_fixed, capacity, has_copy, copy_slot, live_count, slot_rows):
    row_count = route_ids.shape[0]
    slot_count = capacity.shape[0]
    slot_range = jnp.arange(slot_count, dtype=jnp.int32)
    is_live = route_ids < live_count
    onehot = route_ids[:, :, None] == slot_range[None, None, :]
    doubled = jnp.any(onehot & has_copy[None, None, :], axis=2)
    copy_of = jnp.sum(jnp.where(onehot, copy_slot[None, None, :], 0), axis=2)
    odd_row = (jnp.arange(row_count, dtype=jnp.int32) % 2 == 1)[:, None]
    slot_of = jnp.where(doubled & odd_row, copy_of, jnp.where(is_live, route_ids, 0))
    flat_slot = slot_of.reshape(-1)
    flat_live = is_live.reshape(-1)
    member = ((flat_slot[:, None] == slot_range[None, :]) & flat_live[:, None]).astype(jnp.int32)
    before = jnp.cumsum(member, axis=0) - member
    position = jnp.sum(before * member, axis=1)
    allowed = jnp.sum(member * capacity[None, :], axis=1)
    kept_pair = flat_live & (position < allowed)
    target = flat_slot * slot_rows + position
    weight = jnp.where(kept_pair, gate_fixed.reshape(-1).astype(jnp.float32) * GATE_UNIT, 0.0)
    return (target, kept_pair, weight)


def tables(target, kept_pair, weight, row_count, table_width):
    column = jnp.arange(table_width, dtype=jnp.int32)
    matches = (target[:, None] == column[None, :]) & kept_pair[:, None]
    chosen = jnp.sum(matches.astype(jnp.int32).reshape(row_count, -1, table_width), axis=1)
    mixing = jnp.sum(
        (matches.astype(jnp.float32) * weight[:, None]).reshape(row_count, -1, table_width), axis=1
    )
    return (chosen, mixing)


def per_device_general(
    tokens, route_ids, gate_fixed, capacity, placement, gate_weight, up_weight, down_weight
):
    dev_count = lax.axis_size("expert")
    group_size = FF_W // HID_DEV
    slot_count = dev_count // group_size
    live_count = slot_count - placement.shape[0]
    row_count, model_width = tokens.shape
    has_copy, copy_slot, source_slot = slot_tables(placement, slot_count)
    target, kept_pair, weight = assign(
        route_ids, gate_fixed, capacity, has_copy, copy_slot, live_count, CAP
    )
    chosen, mixing = tables(target, kept_pair, weight, row_count, slot_count * CAP)
    slot_range = jnp.arange(slot_count, dtype=jnp.int32)
    owner_table = (source_slot[None, :] == slot_range[:, None]) & (
        source_slot[None, :] != slot_range[None, :]
    )
    gate_mat = gate_weight[0]
    up_mat = up_weight[0]
    down_mat = down_weight[0]
    picked = jnp.dot(
        chosen.T.astype(jnp.bfloat16), tokens, preferred_element_type=jnp.float32
    ).astype(jnp.bfloat16)
    slotted = picked.reshape(slot_count, CAP, model_width)
    block_rows = 2 * CAP
    extra = jnp.dot(
        owner_table.astype(jnp.bfloat16),
        slotted.reshape(slot_count, CAP * model_width),
        preferred_element_type=jnp.float32,
    )
    extra = extra.astype(jnp.bfloat16).reshape(slot_count, CAP, model_width)
    slotted = jnp.concatenate((slotted, extra), axis=1)
    outgoing = jnp.broadcast_to(
        slotted[:, None], (slot_count, group_size, block_rows, model_width)
    ).reshape(dev_count, block_rows, model_width)
    arrived = lax.all_to_all(outgoing, "expert", split_axis=0, concat_axis=0, tiled=True)
    flat_rows = arrived.reshape(-1, model_width)
    gate_val = jnp.dot(flat_rows, gate_mat, preferred_element_type=jnp.float32)
    up_val = jnp.dot(flat_rows, up_mat, preferred_element_type=jnp.float32)
    hidden = (jax.nn.silu(gate_val) * up_val).astype(jnp.bfloat16)
    partial_value = lax.dot_general(
        hidden, down_mat, (((1,), (1,)), ((), ())), preferred_element_type=jnp.float32
    )
    partial_value = partial_value.astype(jnp.bfloat16).reshape(
        arrived.shape[0], arrived.shape[1], model_width
    )
    returned = lax.all_to_all(partial_value, "expert", split_axis=0, concat_axis=0, tiled=True)
    summed = jnp.sum(
        returned.reshape(slot_count, group_size, block_rows, model_width), axis=1, dtype=jnp.float32
    )
    own_out = summed[:, :CAP]
    copy_out = summed[:, CAP:].reshape(slot_count, CAP * model_width)
    copy_back = jnp.dot(
        owner_table.T.astype(jnp.float32), copy_out, precision=lax.Precision.HIGHEST
    ).reshape(slot_count, CAP, model_width)
    is_landing = jnp.any(owner_table, axis=0)
    summed = jnp.where(is_landing[:, None, None], copy_back, own_out)
    combined = jnp.dot(
        mixing, summed.reshape(slot_count * CAP, model_width), precision=lax.Precision.HIGHEST
    )
    return combined.astype(jnp.bfloat16)

MIB = 1024 * 1024


def route_kernel(route_ref, gate_ref, cap_ref, tokens_ref, picked_ref, mix_ref, held, sem):
    row_count = held.shape[0]
    fetch = pltpu.make_async_copy(tokens_ref, held, sem)
    fetch.start()
    hit = route_ref[...] == 0
    member = jnp.sum(jnp.where(hit, 1.0, 0.0), axis=1, keepdims=True)
    fixed = jnp.sum(jnp.where(hit, gate_ref[...], 0), axis=1, keepdims=True)
    shape = (row_count, 128)
    weight = jnp.broadcast_to(fixed.astype(jnp.float32) * GATE_UNIT, shape)
    member = jnp.broadcast_to(member, shape)
    row = lax.broadcasted_iota(jnp.int32, (row_count, row_count), 0)
    col = lax.broadcasted_iota(jnp.int32, (row_count, row_count), 1)
    earlier = jnp.where((col < row) & (((row - col) & 1) == 0), 1.0, 0.0).astype(jnp.bfloat16)
    before = jnp.dot(earlier, member.astype(jnp.bfloat16), preferred_element_type=jnp.float32)
    token = lax.broadcasted_iota(jnp.int32, shape, 0)
    odd = (token & 1) == 1
    limit = jnp.where(odd, cap_ref[1], cap_ref[0]).astype(jnp.float32)
    kept = (member > 0.5) & (before < limit)
    spots = []
    for place in range(CAP):
        here = kept & (before == float(place))
        mix_ref[place] = jnp.where(here, weight, 0.0)
        for slot in range(2):
            mine = here & (odd if slot == 1 else jnp.logical_not(odd))
            spots.append(jnp.max(jnp.where(mine, token, -1), axis=0, keepdims=True))
    spots = [spots[place * 2 + slot][0, 0] for slot in range(2) for place in range(CAP)]
    fetch.wait()
    lines = lax.broadcasted_iota(jnp.int32, (16, 1), 0)
    rows = []
    for spot in spots:
        base = pl.multiple_of((jnp.maximum(spot, 0) // 16) * 16, 16)
        block = held[pl.ds(base, 16), :].astype(jnp.float32)
        rows.append(jnp.sum(jnp.where(lines == spot - base, block, 0.0), axis=0, keepdims=True))
    picked_ref[...] = jnp.concatenate(rows, axis=0).astype(jnp.bfloat16)


def expert_kernel(*refs):
    pieces = refs[:8]
    gate_a, gate_b, up_a, up_b, down_a, down_b = refs[8:14]
    outs = refs[14:22]
    rows_ref = refs[22]
    width = rows_ref.shape[1]
    for pair in range(4):
        both = jnp.concatenate(
            [pieces[2 * pair][...].astype(jnp.float32), pieces[2 * pair + 1][...].astype(jnp.float32)], axis=0
        )
        rows_ref[pl.ds(8 * pair, 8), :] = both
    step = 256
    acc_a = jnp.zeros((32, 2 * HID_DEV), jnp.float32)
    acc_b = jnp.zeros((32, 2 * HID_DEV), jnp.float32)
    for start in range(0, width, step):
        part = pl.ds(start, step)
        left = rows_ref[:, part].astype(jnp.bfloat16)
        wa = jnp.concatenate([gate_a[part, :], up_a[part, :]], axis=1)
        wb = jnp.concatenate([gate_b[part, :], up_b[part, :]], axis=1)
        acc_a = acc_a + jnp.dot(left, wa, preferred_element_type=jnp.float32)
        acc_b = acc_b + jnp.dot(left, wb, preferred_element_type=jnp.float32)
    hidden = []
    for acc in (acc_a, acc_b):
        gate_val = acc[:, :HID_DEV]
        up_val = acc[:, HID_DEV:]
        hidden.append((gate_val / (1.0 + jnp.exp(-gate_val)) * up_val).astype(jnp.bfloat16))
    hidden = jnp.concatenate(hidden, axis=1)
    for start in range(0, width, step):
        part = pl.ds(start, step)
        down = jnp.concatenate([down_a[part, :], down_b[part, :]], axis=1)
        value = lax.dot_general(
            hidden, down, (((1,), (1,)), ((), ())), preferred_element_type=jnp.float32
        )
        for index in range(8):
            outs[index][:, part] = value[4 * index : 4 * index + 4].astype(jnp.bfloat16)


def combine_kernel(serves_ref, own, from_2, from_4, from_6, folded, mix_ref, out_ref, built, sems):
    serves = serves_ref[0] > 0
    total = own[...].astype(jnp.float32)
    for ref in (from_2, from_4, from_6):
        total = total + ref[...].astype(jnp.float32)
    total = jnp.where(serves, total, folded[...].astype(jnp.float32))
    width = total.shape[1]
    odd = (lax.broadcasted_iota(jnp.int32, (16, 1), 0) & 1) == 1
    lanes = [
        jnp.where(odd, total[CAP + place : CAP + place + 1], total[place : place + 1])
        for place in range(CAP)
    ]
    copies = []
    for block in range(out_ref.shape[0] // 16):
        part = pl.ds(16 * block, 16)
        value = mix_ref[0, part, :1] * lanes[0] + mix_ref[1, part, :1] * lanes[1]
        built[part, :] = value.astype(jnp.bfloat16)
        copies.append(pltpu.make_async_copy(built.at[part], out_ref.at[part], sems.at[block]))
        copies[-1].start()
    for copy in copies:
        copy.wait()


def per_device_pair(
    tokens, route_ids, gate_fixed, capacity, placement, gate_weight, up_weight, down_weight
):
    dev_count = lax.axis_size("expert")
    row_count, model_width = tokens.shape
    vmem = pl.BlockSpec(memory_space=pltpu.VMEM)
    smem = pl.BlockSpec(memory_space=pltpu.SMEM)
    anywhere = pl.BlockSpec(memory_space=pl.ANY)

    def swap(value, offset):
        return lax.ppermute(value, "expert", [(i, i ^ offset) for i in range(dev_count)])

    picked, mix = pl.pallas_call(
        route_kernel,
        out_shape=(
            jax.ShapeDtypeStruct((2 * CAP, model_width), jnp.bfloat16),
            jax.ShapeDtypeStruct((CAP, row_count, 128), jnp.float32),
        ),
        in_specs=[vmem, vmem, smem, anywhere],
        out_specs=(vmem, vmem),
        scratch_shapes=[
            pltpu.VMEM((row_count, model_width), jnp.bfloat16),
            pltpu.SemaphoreType.DMA,
        ],
        compiler_params=pltpu.CompilerParams(vmem_limit_bytes=16 * MIB),
        name="route",
    )(route_ids, gate_fixed, capacity, tokens)
    gate_a, up_a, down_a = gate_weight[0], up_weight[0], down_weight[0]
    gate_b, up_b, down_b = (swap(value, 1) for value in (gate_a, up_a, down_a))
    fold = swap(picked, 8)
    own_pieces = [picked] + [swap(picked, k) for k in (2, 4, 6)]
    fold_pieces = [fold] + [swap(fold, k) for k in (2, 4, 6)]
    piece = jax.ShapeDtypeStruct((2 * CAP, model_width), jnp.bfloat16)
    outs = pl.pallas_call(
        expert_kernel,
        out_shape=(piece,) * 8,
        in_specs=[vmem] * 14,
        out_specs=(vmem,) * 8,
        scratch_shapes=[pltpu.VMEM((32, model_width), jnp.float32)],
        compiler_params=pltpu.CompilerParams(vmem_limit_bytes=24 * MIB),
        name="experts",
    )(*own_pieces, *fold_pieces, gate_a, gate_b, up_a, up_b, down_a, down_b)
    own_out, fold_out = outs[:4], outs[4:]
    fold_back = [swap(fold_out[i], k) for i, k in ((1, 2), (2, 4), (3, 6))]
    own_back = [swap(own_out[i], k) for i, k in ((1, 2), (2, 4), (3, 6))]
    fold_sum = fold_out[0].astype(jnp.float32)
    for value in fold_back:
        fold_sum = fold_sum + value.astype(jnp.float32)
    returned = swap(fold_sum.astype(jnp.bfloat16), 8)
    serves = (lax.axis_index("expert") < dev_count // 2).astype(jnp.int32).reshape(1)
    return pl.pallas_call(
        combine_kernel,
        out_shape=jax.ShapeDtypeStruct((row_count, model_width), jnp.bfloat16),
        in_specs=[smem] + [vmem] * 6,
        out_specs=anywhere,
        scratch_shapes=[
            pltpu.VMEM((row_count, model_width), jnp.bfloat16),
            pltpu.SemaphoreType.DMA((row_count // 16,)),
        ],
        compiler_params=pltpu.CompilerParams(vmem_limit_bytes=16 * MIB),
        name="combine",
    )(serves, own_out[0], *own_back, returned, mix)


def per_device(
    tokens, route_ids, gate_fixed, capacity, placement, gate_weight, up_weight, down_weight
):
    group_size = FF_W // HID_DEV
    pair = lax.axis_size("expert") == 2 * group_size and placement.shape[0] == 1 and group_size == 8
    step = per_device_pair if pair else per_device_general
    return step(
        tokens, route_ids, gate_fixed, capacity, placement, gate_weight, up_weight, down_weight
    )


def solution(mesh):
    in_specs = (
        P(("groups", "expert"), None),
        P(("groups", "expert"), None),
        P(("groups", "expert"), None),
        P("groups"),
        P("groups", None),
        P("expert", None, None),
        P("expert", None, None),
        P("expert", None, None),
    )
    out_specs = P(("groups", "expert"), None)
    return jax.shard_map(
        per_device, mesh=mesh, in_specs=in_specs, out_specs=out_specs, check_vma=False
    )
```
